256 devices in a mesh: space: 16 (over y, x), latent: 16 (over z, core).
Axes of the slice: x: 4, y: 4, z: 8, core: 2. Of those that a mesh axis runs over, the one named last changes fastest.
Arguments:
- points: bfloat16 [131072, 768], P(('space', 'latent')), may hold values from -6 to 6
- nbr_holder: int32 [4096, 32, 1], P(('space', 'latent')), may hold values from 0 to 15; in each aligned block of 512 rows (0 to 511, 512 to 1023, ..., all dimensions but the last counted through in order) at most 96 rows name the same one
- nbr_local: int32 [4096, 32], P(('space', 'latent')), may hold values from 0 to 511
- nbr_count: int32 [4096], P(('space', 'latent')), may hold values from 16 to 32
- w_in: bfloat16 [768, 768], replicated, may hold values from -0.21875 to 0.21875
- b_in: float32 [768], replicated, may hold values from -3 to 3
- w_out: bfloat16 [768, 768], replicated, may hold values from -0.21875 to 0.21875
- b_out: float32 [768], replicated, may hold values from -2 to 2
- gain_latent: float32 [768], replicated, may hold values from 0.1 to 1.9
- w_query: bfloat16 [768, 768], replicated, may hold values from -0.21875 to 0.21875
- w_key: bfloat16 [768, 768], replicated, may hold values from -0.21875 to 0.21875
- w_value: bfloat16 [768, 768], replicated, may hold values from -0.21875 to 0.21875
- w_mix: bfloat16 [768, 768], replicated, may hold values from -0.21875 to 0.21875
- latent_temp: float32 [12], replicated, may hold values from 8 to 24
- gain_keys: float32 [768], replicated, may hold values from 0.1 to 1.9
- d_query: bfloat16 [768, 768], replicated, may hold values from -0.21875 to 0.21875
- d_key: bfloat16 [768, 768], replicated, may hold values from -0.21875 to 0.21875
- d_value: bfloat16 [768, 768], replicated, may hold values from -0.21875 to 0.21875
- decoder_temp: float32 [12], replicated, may hold values from 8 to 24
- gain_out: float32 [768], replicated, may hold values from 0.1 to 1.9
- w_head: bfloat16 [4, 768], replicated, may hold values from -0.21875 to 0.21875
- query_embed: bfloat16 [65536, 768], P(('space', 'latent')), may hold values from -6 to 6
Outputs:
- latent_out: bfloat16 [4096, 768], P(('space', 'latent'))
- fields: float32 [4, 65536], P(None, ('space', 'latent'))
The draws below stay inside these ranges and needn't reach their ends.
Inputs may be any that keep to these rules, and one draw needn't show every extreme that they name: `nbr_holder`: among the 512 slots of one device's supernodes, at most 96 name any one holder, and in some device's slots one holder is named exactly 96 times.
All inputs are finite; a program needn't handle non-finite values.
Results may differ from the reference program's by a relative error of at most 0.015.
Values may be sent and summed in bfloat16 or wider, within the bound.
No kernel may reach another device: no remote copies, remote signals or barrier semaphores. Data moves between devices by JAX's collectives and lax.ppermute only.
A program may use at most 192 MiB of HBM per device.

```python
import math
import jax
import jax.numpy as jnp
import numpy as np
from jax import lax

D = 768
HEADS = 12
C_OUT = 4
K = 32
P_DEV = 512
S_DEV = 16
Q_DEV = 256
CAP = 96
POINTS = 131072
S = 4096
QUERIES = 65536
N_LATENT = 16


def draw_points(key, part):
    key = jax.random.fold_in(key, 11)
    noise_key, offset_key = jax.random.split(key)
    slab_count = POINTS // (P_DEV * N_LATENT)
    block_rows = P_DEV // S_DEV
    noise_part = jax.random.normal(noise_key, (slab_count, N_LATENT, S_DEV, block_rows, D), jnp.float32)
    offset = 1.5 * jax.random.normal(offset_key, (slab_count, 1, S_DEV, 1, D), jnp.float32)
    values = jnp.clip(noise_part + offset, -6.0, 6.0)
    return values.reshape(POINTS, D).astype(jnp.bfloat16)


def draw_nbr_local(key, part):
    key = jax.random.fold_in(key, 12)
    near_key, far_key, pick_key = jax.random.split(key, 3)
    block_rows = P_DEV // S_DEV
    super_index = jnp.arange(S, dtype=jnp.int32) % S_DEV
    nearby = super_index[:, None] * block_rows + jax.random.randint(near_key, (S, K), 0, block_rows, dtype=jnp.int32)
    anywhere = jax.random.randint(far_key, (S, K), 0, P_DEV, dtype=jnp.int32)
    picked = jax.random.randint(pick_key, (S, K), 0, 4, dtype=jnp.int32)
    chosen = jnp.where(picked == 0, anywhere, nearby)
    chosen = chosen.at[0, 0].set(0).at[S - 1, 0].set(P_DEV - 1)
    return chosen.astype(jnp.int32)


def with_ends(array, rng, low, top_value):
    dims = array.shape
    place = [jax.random.randint(jax.random.fold_in(rng, axis), (), 0, dims[axis]) for axis in range(len(dims))]
    array = array.at[tuple(place)].set(low)
    longest = dims.index(max(dims))
    place[longest] = (place[longest] + 1) % dims[longest]
    return array.at[tuple(place)].set(top_value)


def steps_of(own_key, extent, shards, low, largest):
    level, own = 1.0, jax.random.fold_in(own_key, 6)
    for axis_at, shards_of in shards:
        draws = jnp.exp(jax.random.uniform(jax.random.fold_in(own, axis_at), (shards_of,), jnp.float32, low / len(shards), largest / len(shards)))
        level = level * jnp.repeat(draws, extent[axis_at] // shards_of).reshape([-1 if axis == axis_at else 1 for axis in range(len(extent))])
    return level


def deal_out(stream_key, own, number, rows, count, top, limit, lean):
    order = jax.random.permutation(stream_key, count)
    crowded, usual = portions_of(count, rows * top, limit, lean, True), portions_of(count, rows * top, limit, lean, False)
    places = jnp.arange(count)

    def named(lengths, turn):
        used = int((lengths > 0).sum())
        fixed = max(1, used // 4)
        moved = fixed + (places - fixed + turn * (used - fixed)) % max(1, count - fixed)
        return jnp.zeros((count,), jnp.int32).at[order[jnp.where(places < fixed, places, moved)]].set(jnp.asarray(lengths, jnp.int32))

    lengths = jnp.where(number % 4 == 0, named(crowded, number // 4), named(usual, number - number // 4 - 1))
    mixed = jax.random.permutation(jax.random.fold_in(own, 3), count)
    giver, receiver = mixed[0:count // 2 * 2:2], mixed[1:count // 2 * 2:2]
    slack = jnp.minimum(lengths[giver] - 1, limit - lengths[receiver]) // 2
    slack = jnp.where((giver == order[0]) | (receiver == order[0]) | (lengths[receiver] == 0), 0, jnp.maximum(slack, 0))
    moved = jax.random.randint(jax.random.fold_in(own, 4), (count // 2,), 0, 1 << 20) % (slack + 1)
    lengths = lengths.at[giver].add(-moved).at[receiver].add(moved)
    items = jnp.searchsorted(jnp.cumsum(lengths), jnp.arange(rows * top), side="right").astype(jnp.int32)
    table = items.reshape(top, rows).T
    table = table[jax.random.permutation(jax.random.fold_in(own, 1), rows)]
    turn = jax.random.randint(jax.random.fold_in(own, 2), (rows, 1), 0, top)
    return jnp.take_along_axis(table, (jnp.arange(top)[None, :] + turn) % top, axis=1)


def portions_of(count, total, limit, slope, full):
    weights = [(1 << 20) // math.isqrt(grade ** slope) + 1 for grade in range(1, count + 1)]
    largest = limit if full else min(limit, max(-(-total // count), total * weights[0] // sum(weights)))
    least = 1 if total - largest >= count - 1 else 0
    holding, surplus = [largest] + [least] * (count - 1), total - largest - least * (count - 1)
    while surplus > 0:
        movable = [i for i in range(1, count) if holding[i] < largest] or [i for i in range(1, count) if holding[i] < limit]
        pool, remaining = sum([weights[i] for i in movable]), surplus
        for i in movable:
            more = min(limit - holding[i], max(1, remaining * weights[i] // pool), surplus)
            holding[i] = holding[i] + more
            surplus = surplus - more
    return np.array(holding)


def gaussian(own_key, extent, width, bound, shards=(), kind=jnp.bfloat16):
    result = jax.random.normal(own_key, extent, jnp.float32) * width
    if len(shards) > 0:
        result = steps_of(own_key, extent, shards, -0.22, 0.18) * result
    return jnp.clip(result, min=-bound, max=bound).astype(kind)


def setup_inputs(seed: int = 0) -> dict:
    seeds = jax.random.split(jax.random.key(seed), 23)
    points = draw_points(jax.random.fold_in(seeds[22], 71), 0)
    nbr_holder_keys = jax.random.split(jax.random.fold_in(seeds[1], 1), S * K // (S_DEV * K))
    nbr_holder_turns = jax.random.permutation(jax.random.fold_in(seeds[1], 3), S * K // (S_DEV * K))
    nbr_holder = jax.vmap(lambda own, number: deal_out(jax.random.fold_in(seeds[1], 2), own, number, S_DEV * K, N_LATENT, 1, CAP, 2))(nbr_holder_keys, nbr_holder_turns).reshape((S, K, 1))
    nbr_local = draw_nbr_local(jax.random.fold_in(seeds[22], 71), 0)
    nbr_count = with_ends(jax.random.randint(seeds[3], (S,), K // 2, K + 1), jax.random.fold_in(seeds[3], 1), K // 2, K).astype(jnp.int32)
    w_in = gaussian(seeds[4], (D, D), D ** -0.5, 0.21875)
    b_in = gaussian(seeds[5], (D,), 0.5, 3.0, (), jnp.float32)
    w_out = gaussian(seeds[6], (D, D), D ** -0.5, 0.21875)
    b_out = gaussian(seeds[7], (D,), 0.3, 2.0, (), jnp.float32)
    gain_latent = jnp.clip(1.0 + 0.18 * jax.random.normal(seeds[8], (D,), jnp.float32), 0.1, 1.9)
    w_query = gaussian(seeds[9], (D, D), D ** -0.5, 0.21875)
    w_key = gaussian(seeds[10], (D, D), D ** -0.5, 0.21875)
    w_value = gaussian(seeds[11], (D, D), D ** -0.5, 0.21875)
    w_mix = gaussian(seeds[12], (D, D), D ** -0.5, 0.21875)
    latent_temp = jnp.clip(jnp.exp(jax.random.uniform(seeds[13], (HEADS,), jnp.float32, math.log(8.0), math.log(24.0))), 8.0, 24.0)
    gain_keys = jnp.clip(1.0 + 0.18 * jax.random.normal(seeds[14], (D,), jnp.float32), 0.1, 1.9)
    d_query = gaussian(seeds[15], (D, D), D ** -0.5, 0.21875)
    d_key = gaussian(seeds[16], (D, D), D ** -0.5, 0.21875)
    d_value = gaussian(seeds[17], (D, D), D ** -0.5, 0.21875)
    decoder_temp = jnp.clip(jnp.exp(jax.random.uniform(seeds[18], (HEADS,), jnp.float32, math.log(8.0), math.log(24.0))), 8.0, 24.0)
    gain_out = jnp.clip(1.0 + 0.18 * jax.random.normal(seeds[19], (D,), jnp.float32), 0.1, 1.9)
    w_head = gaussian(seeds[20], (C_OUT, D), D ** -0.5, 0.21875)
    query_embed = gaussian(seeds[21], (QUERIES, D), 1.0, 6.0, ((0, 256),))
    return {"points": points, "nbr_holder": nbr_holder, "nbr_local": nbr_local, "nbr_count": nbr_count, "w_in": w_in, "b_in": b_in, "w_out": w_out, "b_out": b_out, "gain_latent": gain_latent, "w_query": w_query, "w_key": w_key, "w_value": w_value, "w_mix": w_mix, "latent_temp": latent_temp, "gain_keys": gain_keys, "d_query": d_query, "d_key": d_key, "d_value": d_value, "decoder_temp": decoder_temp, "gain_out": gain_out, "w_head": w_head, "query_embed": query_embed}


def layer_norm(inputs, gain_vec):
    inputs = inputs.astype(jnp.float32)
    centred = inputs - lax.optimization_barrier(jnp.mean(inputs, axis=-1, keepdims=True))
    spread = lax.optimization_barrier(jnp.mean(centred * centred, axis=-1, keepdims=True))
    return centred * lax.rsqrt(spread + 1e-05) * gain_vec

def head_norm(inputs, head_count):
    shaped = inputs.reshape(inputs.shape[0], head_count, -1)
    scaled = shaped * lax.rsqrt(lax.optimization_barrier(jnp.mean(shaped * shaped, axis=-1, keepdims=True)) + 1e-06)
    return scaled.reshape(inputs.shape[0], -1).astype(jnp.bfloat16)

def attend(queries, keys_all, values_all, temps, head_count):
    head_size = queries.shape[1] // head_count
    head_query = queries.astype(jnp.float32).reshape(queries.shape[0], head_count, head_size)
    head_keys = keys_all.astype(jnp.float32).reshape(keys_all.shape[0], head_count, head_size)
    head_values = values_all.astype(jnp.float32).reshape(values_all.shape[0], head_count, head_size)
    scores = jnp.einsum('qhd,khd->qhk', head_query, head_keys) * (temps / head_size)[None, :, None]
    weights = jnp.exp(scores - temps[None, :, None])
    totals = lax.optimization_barrier(jnp.sum(weights, axis=-1))
    rounded = lax.optimization_barrier(weights.astype(jnp.bfloat16)).astype(jnp.float32)
    summed = jnp.einsum('qhk,khd->qhd', rounded, head_values)
    return (summed / totals[:, :, None]).reshape(queries.shape[0], -1)

def reference(points, nbr_holder, nbr_local, nbr_count, w_in, b_in, w_out, b_out, gain_latent, w_query, w_key, w_value, w_mix, latent_temp, gain_keys, d_query, d_key, d_value, decoder_temp, gain_out, w_head, query_embed):
    super_rows = jnp.arange(S, dtype=jnp.int32)
    slab_ids = super_rows // S_DEV // N_LATENT
    point_index = (slab_ids[:, None] * N_LATENT + nbr_holder[:, :, 0]) * P_DEV + nbr_local
    gathered = points[point_index.reshape(-1).astype(jnp.int32)]
    hidden = jax.nn.gelu(jnp.dot(gathered, w_in, preferred_element_type=jnp.float32) + b_in).astype(jnp.bfloat16)
    messages = jnp.dot(hidden, w_out, preferred_element_type=jnp.float32).reshape(S, K, D)
    is_live = (jnp.arange(K, dtype=jnp.int32)[None, :] < nbr_count[:, None]).astype(jnp.float32)
    summed = lax.optimization_barrier(jnp.sum(messages * is_live[:, :, None], axis=1))
    pooled = (summed / nbr_count[:, None].astype(jnp.float32) + b_out).astype(jnp.bfloat16)
    normed = layer_norm(pooled, gain_latent).astype(jnp.bfloat16)
    lat_q = head_norm(jnp.dot(normed, w_query, preferred_element_type=jnp.float32), HEADS)
    lat_k = head_norm(jnp.dot(normed, w_key, preferred_element_type=jnp.float32), HEADS)
    lat_v = jnp.dot(normed, w_value, preferred_element_type=jnp.float32).astype(jnp.bfloat16)
    attended = attend(lat_q, lat_k, lat_v, latent_temp, HEADS).astype(jnp.bfloat16)
    latent_out = (pooled.astype(jnp.float32) + jnp.dot(attended, w_mix, preferred_element_type=jnp.float32)).astype(jnp.bfloat16)
    keyed = layer_norm(latent_out, gain_keys).astype(jnp.bfloat16)
    dec_k = head_norm(jnp.dot(keyed, d_key, preferred_element_type=jnp.float32), HEADS)
    dec_v = jnp.dot(keyed, d_value, preferred_element_type=jnp.float32).astype(jnp.bfloat16)

    def decode(query_block):
        dec_q = head_norm(jnp.dot(query_block, d_query, preferred_element_type=jnp.float32), HEADS)
        decoded = attend(dec_q, dec_k, dec_v, decoder_temp, HEADS)
        final_rows = layer_norm(decoded, gain_out).astype(jnp.bfloat16)
        return lax.dot_general(w_head, final_rows, (((1,), (1,)), ((), ())), preferred_element_type=jnp.float32)
    blocks = query_embed.reshape(-1, Q_DEV, D)
    fields = lax.map(decode, blocks)
    fields = fields.transpose(1, 0, 2).reshape(C_OUT, -1)
    return (latent_out, fields)
```

```python
import functools

import jax
import jax.numpy as jnp
from jax import lax
from jax.experimental import pallas as pl
from jax.experimental.pallas import tpu as pltpu
from jax.sharding import Mesh, PartitionSpec as P

HEADS = 12
HEAD = 64
D = 768
LOG2E = 1.4426950408889634
AXES = ("y", "x", "z", "c")
SIZE = {"y": 4, "x": 4, "z": 8, "c": 2}
BF = jnp.bfloat16
F32 = jnp.float32


def dot(a, b):
    return jnp.dot(a, b, preferred_element_type=F32)


def dot_nt(a, b):
    return lax.dot_general(a, b, (((1,), (1,)), ((), ())), preferred_element_type=F32)


def split(x):
    hi = x.astype(BF)
    return hi, (x - hi.astype(F32)).astype(BF)


def head_map(rows_first):
    shape = (D, 128) if rows_first else (128, D)
    a = lax.broadcasted_iota(jnp.int32, shape, 0)
    b = lax.broadcasted_iota(jnp.int32, shape, 1)
    hit = (lax.shift_right_logical(a, 6) == b) if rows_first else (lax.shift_right_logical(b, 6) == a)
    return jnp.where(hit, 1.0, 0.0).astype(BF)


def head_norm(u):
    ms = sum(dot(part, head_map(True)) for part in split(u * u)) * (1.0 / HEAD)
    r = lax.rsqrt(ms + 1e-6)
    scale = sum(dot(part, head_map(False)) for part in split(r))
    return u * scale


def layer_norm(x, gain):
    x = x.astype(F32)
    centred = x - jnp.mean(x, axis=-1, keepdims=True)
    spread = jnp.mean(centred * centred, axis=-1, keepdims=True)
    return centred * lax.rsqrt(spread + 1e-5) * gain


def call(kernel, out_shape, *args, scratch=(), smem=(), flops=0, vmem=48):
    specs = [
        pl.BlockSpec(memory_space=pltpu.SMEM if i in smem else pltpu.VMEM) for i in range(len(args))
    ]
    many = isinstance(out_shape, (list, tuple))
    out_specs = (
        [pl.BlockSpec(memory_space=pltpu.VMEM) for _ in out_shape]
        if many
        else pl.BlockSpec(memory_space=pltpu.VMEM)
    )
    nbytes = sum(a.size * a.dtype.itemsize for a in args)
    return pl.pallas_call(
        kernel,
        out_shape=out_shape,
        in_specs=specs,
        out_specs=out_specs,
        scratch_shapes=list(scratch),
        cost_estimate=pl.CostEstimate(flops=flops, bytes_accessed=nbytes, transcendentals=0),
        compiler_params=pltpu.CompilerParams(vmem_limit_bytes=vmem * 1024 * 1024),
    )(*args)


def message_kernel(points, w_in, b_in, w_out, hi, lo):
    hidden = jax.nn.gelu(dot(points[...], w_in[...]) + b_in[...]).astype(BF)
    hi[...], lo[...] = split(dot(hidden, w_out[...]))


def partial_kernel(idx, hi, lo, out):
    codes = idx[...]
    rows, slots = codes.shape
    points = hi.shape[0]
    lane = lax.broadcasted_iota(jnp.int32, (rows, points), 1)
    counts = jnp.zeros((rows, points), F32)
    for j in range(slots):
        counts += jnp.where(codes[:, j : j + 1] == lane, 1.0, 0.0)
    counts = counts.astype(BF)
    out[...] = (dot(counts, hi[...]) + dot(counts, lo[...])).astype(BF)


def pool_kernel(parts, count, b_out, pooled):
    rows = pooled.shape[0]
    total = jnp.zeros((rows, D), F32)
    for i in range(parts.shape[0] // rows):
        total += parts[i * rows : (i + 1) * rows, :].astype(F32)
    pooled[...] = (total / count[...] + b_out[...]).astype(BF)


def latent_query_kernel(pooled, gain, w, scale, out):
    normed = layer_norm(pooled[...], gain[...]).astype(BF)
    out[...] = (head_norm(dot(normed, w[...])) * scale[...]).astype(BF)


def query_kernel(rows, w, scale, out):
    out[...] = (head_norm(dot(rows[...], w[...])) * scale[...]).astype(BF)


def attend_kernel(n, *refs):
    pieces = refs[:n]
    temps, gain, wk, wv, q, own, part, den, nrm, keys, vals, acc = refs[n:]
    at = 0
    for piece in pieces:
        rows = piece.shape[0]
        nrm[at : at + rows, :] = layer_norm(piece[...], gain[...]).astype(BF)
        at += rows
    total = at
    block = 512
    nq = q.shape[0]

    @pl.loop(0, total // block)
    def _(i):
        here = pl.ds(pl.multiple_of(i * block, block), block)
        keyed = nrm[here, :]
        keys[here, :] = head_norm(dot(keyed, wk[...])).astype(BF)
        vals[here, :] = dot(keyed, wv[...]).astype(BF)

    low = lax.broadcasted_iota(jnp.int32, (1, 128), 1) < HEAD
    den[...] = jnp.zeros(den.shape, F32)
    half = nq // 2

    @pl.loop(0, HEADS // 2)
    def _(pair):
        lanes = pl.ds(pl.multiple_of(pair * 128, 128), 128)
        q_pair = q[:, lanes]
        zero = jnp.zeros((), BF)
        one = jnp.ones((), BF)
        qs = (jnp.where(low, q_pair, zero), jnp.where(low, zero, q_pair))
        shifts = (temps[2 * pair], temps[2 * pair + 1])

        acc[...] = jnp.zeros(acc.shape, F32)

        @pl.loop(0, total // block)
        def _(i):
            here = pl.ds(pl.multiple_of(i * block, block), block)
            k_pair = keys[here, lanes]
            v_pair = vals[here, lanes]
            vs = (jnp.where(low, v_pair, one), jnp.where(low, one, v_pair))
            for h in range(2):
                e = jnp.exp2(dot_nt(qs[h], k_pair) - shifts[h]).astype(BF)
                acc[h] += dot(e, vs[h])

        even, odd = acc[0], acc[1]
        numer = jnp.where(low, even, odd)
        own[:, lanes] = numer[:half]
        part[:, lanes] = numer[half:].astype(BF)
        lane = lax.broadcasted_iota(jnp.int32, (1, 128), 1)
        den[...] += jnp.where(lane == HEAD + pair, even, 0.0) + jnp.where(lane == pair, odd, 0.0)


def den_map():
    a = lax.broadcasted_iota(jnp.int32, (128, D), 0)
    head = lax.shift_right_logical(lax.broadcasted_iota(jnp.int32, (128, D), 1), 6)
    pair = lax.shift_right_logical(head, 1)
    place = jnp.where(jnp.bitwise_and(head, 1) == 0, HEAD + pair, pair)
    return jnp.where(a == place, 1.0, 0.0).astype(BF)


def merged(own, part, den, den_part):
    total = den[...] + den_part[...]
    inverse = 1.0 / jnp.where(total > 0.0, total, 1.0)
    scale = sum(dot(piece, den_map()) for piece in split(inverse))
    return (own[...] + part[...].astype(F32)) * scale


def mix_kernel(own, part, den, den_part, pooled, w, out):
    attended = merged(own, part, den, den_part).astype(BF)
    out[...] = (pooled[...].astype(F32) + dot(attended, w[...])).astype(BF)


def head_kernel(own, part, den, den_part, gain, w, out):
    rows = layer_norm(merged(own, part, den, den_part), gain[...]).astype(BF)
    out[...] = dot_nt(w[...], rows)


def fetch(t, axis, ahead):
    n = SIZE[axis]
    return lax.ppermute(t, axis, [(i, (i - ahead) % n) for i in range(n)])


def gather_z(t):
    n = t.shape[0]
    after, before = fetch(t, "z", 1), fetch(t, "z", -1)
    three = jnp.concatenate([before, t, after], axis=0)
    far = fetch(three, "z", 3)
    back = fetch(three[n:], "z", -3)
    return jnp.concatenate([t, after, far, back, before], axis=0)


def ring(t, axis):
    return [t] + [fetch(t, axis, k) for k in range(1, SIZE[axis])]


def cat(pieces):
    return jnp.concatenate(pieces, axis=0)


def gather_rows(t):
    wide = gather_z(t[:12])
    per = wide.reshape(8, 12, D)
    a = per[:, :6].reshape(48, D)
    b = per[:, 6:].reshape(48, D)
    c = t[12:]
    a = ring(cat(ring(a, "x")), "y")
    b = ring(cat(ring(b, "y")), "x")
    c = ring(cat(ring(cat(ring(c, "x")), "y")), "z")
    return a + b + c


def attend(rows, q, temps, gain, wk, wv):
    nq = q.shape[0]
    total = sum(r.shape[0] for r in rows)
    shapes = [
        jax.ShapeDtypeStruct((nq // 2, D), F32),
        jax.ShapeDtypeStruct((nq // 2, D), BF),
        jax.ShapeDtypeStruct((nq, 128), F32),
    ]
    scratch = [pltpu.VMEM((total, D), BF)] * 3 + [pltpu.VMEM((2, nq, 128), F32)]
    own, part, den = call(
        functools.partial(attend_kernel, len(rows)),
        shapes,
        *rows,
        temps,
        gain,
        wk,
        wv,
        q,
        scratch=scratch,
        smem=(len(rows),),
        flops=4 * total * D * (D + 4 * nq),
    )
    swap = [(0, 1), (1, 0)]
    part = lax.ppermute(part, "c", swap)
    den_part = lax.ppermute(den[nq // 2 :], "c", swap)
    return own, part, den[: nq // 2], den_part


def body(
    points,
    nbr_holder,
    nbr_local,
    nbr_count,
    w_in,
    b_in,
    w_out,
    b_out,
    gain_latent,
    w_query,
    w_key,
    w_value,
    w_mix,
    latent_temp,
    gain_keys,
    d_query,
    d_key,
    d_value,
    decoder_temp,
    gain_out,
    w_head,
    query_embed,
):
    rows_dev, slot_count = nbr_local.shape
    point_rows = points.shape[0]
    queries = query_embed.shape[0]
    swap = [(0, 1), (1, 0)]
    z, c = lax.axis_index("z"), lax.axis_index("c")
    row = lambda v: v.reshape(1, -1)
    shape = jax.ShapeDtypeStruct

    live = lax.broadcasted_iota(jnp.int32, (rows_dev, slot_count), 1) < nbr_count[:, None]
    code = jnp.where(live, nbr_holder[:, :, 0] * point_rows + nbr_local, -1)
    other = lax.ppermute(code, "c", swap)
    chip = jnp.where(c == 0, cat([code, other]), cat([other, code]))
    slab = gather_z(chip)
    slab = lax.dynamic_slice_in_dim(cat([slab, slab]), (8 - z) % 8 * (2 * rows_dev), 16 * rows_dev, 0)
    first = (z * 2 + c) * point_rows
    idx = jnp.where((slab >= first) & (slab < first + point_rows), slab - first, -1)

    hi, lo = call(
        message_kernel,
        [shape((point_rows, D), BF)] * 2,
        points,
        w_in,
        row(b_in),
        w_out,
        flops=4 * point_rows * D * D,
    )
    partial = call(
        partial_kernel, shape((16 * rows_dev, D), BF), idx, hi, lo, flops=64 * rows_dev * point_rows * D
    )
    parts = lax.all_to_all(partial, ("z", "c"), split_axis=0, concat_axis=0, tiled=True)
    pooled = call(
        pool_kernel, shape((rows_dev, D), BF), parts, nbr_count.astype(F32)[:, None], row(b_out)
    )

    per_feature = lambda temp: row(jnp.repeat(temp * (LOG2E / HEAD), HEAD))
    dec_q = call(
        query_kernel,
        shape((queries, D), BF),
        query_embed,
        d_query,
        per_feature(decoder_temp),
        flops=2 * queries * D * D,
    )
    dec_q = cat([dec_q, lax.ppermute(dec_q, "c", swap)])

    lat_rows = gather_rows(pooled)
    lat_q = call(
        latent_query_kernel,
        shape((rows_dev, D), BF),
        pooled,
        row(gain_latent),
        w_query,
        per_feature(latent_temp),
        flops=2 * rows_dev * D * D,
    )
    lat_q = cat([lat_q, lax.ppermute(lat_q, "c", swap)])
    found = attend(lat_rows, lat_q, latent_temp * LOG2E, row(gain_latent), w_key, w_value)
    latent_out = call(mix_kernel, shape((rows_dev, D), BF), *found, pooled, w_mix)

    dec_rows = gather_rows(latent_out)
    found = attend(dec_rows, dec_q, decoder_temp * LOG2E, row(gain_keys), d_key, d_value)
    fields = call(head_kernel, shape((w_head.shape[0], queries), F32), *found, row(gain_out), w_head)
    return (latent_out, fields)


def solution(mesh):
    fine = Mesh(mesh.devices.reshape([SIZE[a] for a in AXES]), AXES)
    rows = P(AXES, None)
    placed = (rows, P(AXES, None, None), rows, P(AXES)) + (P(),) * 17 + (rows,)
    return jax.shard_map(
        body,
        mesh=fine,
        in_specs=placed,
        out_specs=(rows, P(None, AXES)),
        check_vma=False,
    )
```

```python
import functools

import jax
import jax.numpy as jnp
from jax import lax
from jax.experimental import pallas as pl
from jax.experimental.pallas import tpu as pltpu
from jax.sharding import Mesh, PartitionSpec as P

HEADS = 12
HEAD = 64
D = 768
LOG2E = 1.4426950408889634
AXES = ("y", "x", "z", "c")
SIZE = {"y": 4, "x": 4, "z": 8, "c": 2}
BF = jnp.bfloat16
F32 = jnp.float32


def dot(a, b):
    return jnp.dot(a, b, preferred_element_type=F32)


def dot_nt(a, b):
    return lax.dot_general(a, b, (((1,), (1,)), ((), ())), preferred_element_type=F32)


def split(x):
    hi = x.astype(BF)
    return hi, (x - hi.astype(F32)).astype(BF)


def head_map(rows_first):
    shape = (D, 128) if rows_first else (128, D)
    a = lax.broadcasted_iota(jnp.int32, shape, 0)
    b = lax.broadcasted_iota(jnp.int32, shape, 1)
    hit = (lax.shift_right_logical(a, 6) == b) if rows_first else (lax.shift_right_logical(b, 6) == a)
    return jnp.where(hit, 1.0, 0.0).astype(BF)


def head_norm(u):
    ms = sum(dot(part, head_map(True)) for part in split(u * u)) * (1.0 / HEAD)
    r = lax.rsqrt(ms + 1e-6)
    scale = sum(dot(part, head_map(False)) for part in split(r))
    return u * scale


def layer_norm(x, gain):
    x = x.astype(F32)
    centred = x - jnp.mean(x, axis=-1, keepdims=True)
    spread = jnp.mean(centred * centred, axis=-1, keepdims=True)
    return centred * lax.rsqrt(spread + 1e-5) * gain


def call(kernel, out_shape, *args, scratch=(), smem=(), flops=0, vmem=48):
    specs = [
        pl.BlockSpec(memory_space=pltpu.SMEM if i in smem else pltpu.VMEM) for i in range(len(args))
    ]
    many = isinstance(out_shape, (list, tuple))
    out_specs = (
        [pl.BlockSpec(memory_space=pltpu.VMEM) for _ in out_shape]
        if many
        else pl.BlockSpec(memory_space=pltpu.VMEM)
    )
    nbytes = sum(a.size * a.dtype.itemsize for a in args)
    return pl.pallas_call(
        kernel,
        out_shape=out_shape,
        in_specs=specs,
        out_specs=out_specs,
        scratch_shapes=list(scratch),
        cost_estimate=pl.CostEstimate(flops=flops, bytes_accessed=nbytes, transcendentals=0),
        compiler_params=pltpu.CompilerParams(vmem_limit_bytes=vmem * 1024 * 1024),
    )(*args)


def message_kernel(points, w_in, b_in, w_out, hi, lo):
    hidden = jax.nn.gelu(dot(points[...], w_in[...]) + b_in[...]).astype(BF)
    hi[...], lo[...] = split(dot(hidden, w_out[...]))


def partial_kernel(idx, hi, lo, out):
    codes = idx[...]
    rows, slots = codes.shape
    points = hi.shape[0]
    lane = lax.broadcasted_iota(jnp.int32, (rows, points), 1)
    counts = jnp.zeros((rows, points), F32)
    for j in range(slots):
        counts += jnp.where(codes[:, j : j + 1] == lane, 1.0, 0.0)
    counts = counts.astype(BF)
    out[...] = (dot(counts, hi[...]) + dot(counts, lo[...])).astype(BF)


def pool_kernel(parts, count, b_out, pooled):
    rows = pooled.shape[0]
    total = jnp.zeros((rows, D), F32)
    for i in range(parts.shape[0] // rows):
        total += parts[i * rows : (i + 1) * rows, :].astype(F32)
    pooled[...] = (total / count[...] + b_out[...]).astype(BF)


def latent_query_kernel(pooled, gain, w, scale, out):
    normed = layer_norm(pooled[...], gain[...]).astype(BF)
    out[...] = (head_norm(dot(normed, w[...])) * scale[...]).astype(BF)


def query_kernel(rows, w, scale, out):
    out[...] = (head_norm(dot(rows[...], w[...])) * scale[...]).astype(BF)


def project_kernel(n, *refs):
    pieces = refs[:n]
    gain, wk, wv, keys, vals = refs[n:]
    at = 0
    for piece in pieces:
        rows = piece.shape[0]
        keyed = layer_norm(piece[...], gain[...]).astype(BF)
        keys[at : at + rows, :] = head_norm(dot(keyed, wk[...])).astype(BF)
        vals[at : at + rows, :] = dot(keyed, wv[...]).astype(BF)
        at += rows


def attend_kernel(temps, q, keys, vals, own, part):
    nq = q.shape[0]
    half = nq // 2
    lane = lax.broadcasted_iota(jnp.int32, (1, 128), 1)
    low = lane < HEAD
    zero = jnp.zeros((), BF)
    one = jnp.ones((), BF)
    den = jnp.zeros((nq, 128), F32)
    for pair in range(HEADS // 2):
        lanes = slice(pair * 128, pair * 128 + 128)
        q_pair, k_pair, v_pair = q[:, lanes], keys[:, lanes], vals[:, lanes]
        qs = (jnp.where(low, q_pair, zero), jnp.where(low, zero, q_pair))
        vs = (jnp.where(low, v_pair, one), jnp.where(low, one, v_pair))
        found = []
        for h in range(2):
            e = jnp.exp2(dot_nt(qs[h], k_pair) - temps[2 * pair + h]).astype(BF)
            found.append(dot(e, vs[h]))
        numer = jnp.where(low, found[0], found[1])
        own[:, lanes] = numer[:half]
        part[:, lanes] = numer[half:].astype(BF)
        den += jnp.where(lane == HEAD + pair, found[0], 0.0)
        den += jnp.where(lane == pair, found[1], 0.0)
    own[:, D:] = den[:half]
    part[:, D:] = den[half:].astype(BF)


def den_map():
    a = lax.broadcasted_iota(jnp.int32, (128, D), 0)
    head = lax.shift_right_logical(lax.broadcasted_iota(jnp.int32, (128, D), 1), 6)
    pair = lax.shift_right_logical(head, 1)
    place = jnp.where(jnp.bitwise_and(head, 1) == 0, HEAD + pair, pair)
    return jnp.where(a == place, 1.0, 0.0).astype(BF)


def merged(parts):
    whole = sum(p[...].astype(F32) for p in parts)
    den = whole[:, D:]
    inverse = 1.0 / jnp.where(den > 0.0, den, 1.0)
    scale = sum(dot(piece, den_map()) for piece in split(inverse))
    return whole[:, :D] * scale


def mix_kernel(n, *refs):
    pooled, w, out = refs[n:]
    attended = merged(refs[:n]).astype(BF)
    out[...] = (pooled[...].astype(F32) + dot(attended, w[...])).astype(BF)


def head_kernel(n, *refs):
    gain, w, out = refs[n:]
    rows = layer_norm(merged(refs[:n]), gain[...]).astype(BF)
    out[...] = dot_nt(w[...], rows)


def fetch(t, axis, ahead):
    n = SIZE[axis]
    return lax.ppermute(t, axis, [(i, (i - ahead) % n) for i in range(n)])


def gather_z(t):
    n = t.shape[0]
    after, before = fetch(t, "z", 1), fetch(t, "z", -1)
    three = jnp.concatenate([before, t, after], axis=0)
    far = fetch(three, "z", 3)
    back = fetch(three[n:], "z", -3)
    return jnp.concatenate([t, after, far, back, before], axis=0)


def ring(t, axis):
    return [t] + [fetch(t, axis, k) for k in range(1, SIZE[axis])]


def cat(pieces):
    return jnp.concatenate(pieces, axis=0)


def gather_rows(t):
    return ring(gather_z(t), "y")


SWAP = [(0, 1), (1, 0)]


def project(rows, gain, wk, wv):
    total = sum(r.shape[0] for r in rows)
    return call(
        functools.partial(project_kernel, len(rows)),
        [jax.ShapeDtypeStruct((total, D), BF)] * 2,
        *rows,
        gain,
        wk,
        wv,
        flops=4 * total * D * D,
    )


def attend(q, temps, keys, vals):
    half = q.shape[0] // 2
    own, part = call(
        attend_kernel,
        [jax.ShapeDtypeStruct((half, D + 128), F32), jax.ShapeDtypeStruct((half, D + 128), BF)],
        temps,
        q,
        keys,
        vals,
        smem=(0,),
        flops=16 * q.shape[0] * keys.shape[0] * D,
    )
    return own, lax.ppermute(part, "c", SWAP)


def body(
    points,
    nbr_holder,
    nbr_local,
    nbr_count,
    w_in,
    b_in,
    w_out,
    b_out,
    gain_latent,
    w_query,
    w_key,
    w_value,
    w_mix,
    latent_temp,
    gain_keys,
    d_query,
    d_key,
    d_value,
    decoder_temp,
    gain_out,
    w_head,
    query_embed,
):
    rows_dev, slot_count = nbr_local.shape
    point_rows = points.shape[0]
    queries = query_embed.shape[0]
    z, c = lax.axis_index("z"), lax.axis_index("c")
    row = lambda v: v.reshape(1, -1)
    shape = jax.ShapeDtypeStruct

    live = lax.broadcasted_iota(jnp.int32, (rows_dev, slot_count), 1) < nbr_count[:, None]
    code = jnp.where(live, nbr_holder[:, :, 0] * point_rows + nbr_local, -1)
    other = lax.ppermute(code, "c", SWAP)
    chip = jnp.where(c == 0, cat([code, other]), cat([other, code]))
    slab = gather_z(chip)
    slab = lax.dynamic_slice_in_dim(cat([slab, slab]), (8 - z) % 8 * (2 * rows_dev), 16 * rows_dev, 0)
    first = (z * 2 + c) * point_rows
    idx = jnp.where((slab >= first) & (slab < first + point_rows), slab - first, -1)

    hi, lo = call(
        message_kernel,
        [shape((point_rows, D), BF)] * 2,
        points,
        w_in,
        row(b_in),
        w_out,
        flops=4 * point_rows * D * D,
    )
    partial = call(
        partial_kernel, shape((16 * rows_dev, D), BF), idx, hi, lo, flops=64 * rows_dev * point_rows * D
    )
    parts = lax.all_to_all(partial, ("z", "c"), split_axis=0, concat_axis=0, tiled=True)
    pooled = call(
        pool_kernel, shape((rows_dev, D), BF), parts, nbr_count.astype(F32)[:, None], row(b_out)
    )

    per_feature = lambda temp: row(jnp.repeat(temp * (LOG2E / HEAD), HEAD))
    dec_q = call(
        query_kernel,
        shape((queries, D), BF),
        query_embed,
        d_query,
        per_feature(decoder_temp),
        flops=2 * queries * D * D,
    )
    dec_q = cat([dec_q, lax.ppermute(dec_q, "c", SWAP)])
    ahead, behind = fetch(dec_q, "x", 1), fetch(dec_q, "x", -1)
    across = cat([fetch(ahead[:queries], "x", 1), fetch(behind[queries:], "x", -1)])

    lat_q = call(
        latent_query_kernel,
        shape((rows_dev, D), BF),
        pooled,
        row(gain_latent),
        w_query,
        per_feature(latent_temp),
        flops=2 * rows_dev * D * D,
    )
    lat_q = cat(ring(lat_q, "x"))
    lat_q = cat([lat_q, lax.ppermute(lat_q, "c", SWAP)])
    keys, vals = project(gather_rows(pooled), row(gain_latent), w_key, w_value)
    own, part = attend(lat_q, latent_temp * LOG2E, keys, vals)
    both = own + part.astype(F32)
    block = lambda k: both[k * rows_dev : (k + 1) * rows_dev]
    found = [block(0)] + [fetch(block(k).astype(BF), "x", -k) for k in range(1, 4)]
    latent_out = call(
        functools.partial(mix_kernel, 4), shape((rows_dev, D), BF), *found, pooled, w_mix
    )

    keys, vals = project(gather_rows(latent_out), row(gain_keys), d_key, d_value)
    temps = decoder_temp * LOG2E
    half = queries // 2
    own, part = attend(across, temps, keys, vals)
    far = (own + part.astype(F32)).astype(BF)
    onward = fetch(far[:half], "x", -1)
    back = fetch(far[half:], "x", 1)
    own, part = attend(ahead, temps, keys, vals)
    own = own + part.astype(F32)
    to_ahead = fetch(cat([own[:half] + onward.astype(F32), own[half:]]).astype(BF), "x", -1)
    own, part = attend(behind, temps, keys, vals)
    own = own + part.astype(F32)
    to_behind = fetch(cat([own[:half], own[half:] + back.astype(F32)]).astype(BF), "x", 1)
    own, part = attend(dec_q, temps, keys, vals)
    fields = call(
        functools.partial(head_kernel, 4),
        shape((w_head.shape[0], queries), F32),
        own,
        part,
        to_ahead,
        to_behind,
        row(gain_out),
        w_head,
    )
    return (latent_out, fields)


def solution(mesh):
    fine = Mesh(mesh.devices.reshape([SIZE[a] for a in AXES]), AXES)
    rows = P(AXES, None)
    placed = (rows, P(AXES, None, None), rows, P(AXES)) + (P(),) * 17 + (rows,)
    return jax.shard_map(
        body,
        mesh=fine,
        in_specs=placed,
        out_specs=(rows, P(None, AXES)),
        check_vma=False,
    )
```

```python
import functools

import jax
import jax.numpy as jnp
from jax import lax
from jax.experimental import pallas as pl
from jax.experimental.pallas import tpu as pltpu
from jax.sharding import Mesh, PartitionSpec as P

HEADS = 12
HEAD = 64
D = 768
LOG2E = 1.4426950408889634
AXES = ("y", "x", "z", "c")
SIZE = {"y": 4, "x": 4, "z": 8, "c": 2}
BF = jnp.bfloat16
F32 = jnp.float32


def dot(a, b):
    return jnp.dot(a, b, preferred_element_type=F32)


def dot_nt(a, b):
    return lax.dot_general(a, b, (((1,), (1,)), ((), ())), preferred_element_type=F32)


def split(x):
    hi = x.astype(BF)
    return hi, (x - hi.astype(F32)).astype(BF)


def head_norm(u):
    head = lax.shift_right_logical(lax.broadcasted_iota(jnp.int32, (D, 128), 0), 6)
    gather = jnp.where(head == lax.broadcasted_iota(jnp.int32, (D, 128), 1), 1.0, 0.0).astype(BF)
    ms = dot((u * u).astype(BF), gather) * (1.0 / HEAD)
    part = jnp.bitwise_and(lax.broadcasted_iota(jnp.int32, (256, D), 0), 127)
    head = lax.shift_right_logical(lax.broadcasted_iota(jnp.int32, (256, D), 1), 6)
    spread = jnp.where(part == head, 1.0, 0.0).astype(BF)
    return u * dot(jnp.concatenate(split(lax.rsqrt(ms + 1e-6)), axis=1), spread)


def layer_norm(x, gain):
    x = x.astype(F32)
    centred = x - jnp.mean(x, axis=-1, keepdims=True)
    spread = jnp.mean(centred * centred, axis=-1, keepdims=True)
    return centred * lax.rsqrt(spread + 1e-5) * gain


def call(kernel, out_shape, *args, after=(), smem=(), flops=0, vmem=48):
    specs = [
        pl.BlockSpec(memory_space=pltpu.SMEM if i in smem else pltpu.VMEM) for i in range(len(args))
    ]
    many = isinstance(out_shape, (list, tuple))
    out_specs = (
        [pl.BlockSpec(memory_space=pltpu.VMEM) for _ in out_shape]
        if many
        else pl.BlockSpec(memory_space=pltpu.VMEM)
    )
    specs += [pl.BlockSpec(memory_space=pl.ANY)] * len(after)
    nbytes = sum(a.size * a.dtype.itemsize for a in args)

    def run(*refs):
        kernel(*refs[: len(args)], *refs[len(args) + len(after) :])

    return pl.pallas_call(
        run,
        out_shape=out_shape,
        in_specs=specs,
        out_specs=out_specs,
        cost_estimate=pl.CostEstimate(flops=flops, bytes_accessed=nbytes, transcendentals=0),
        compiler_params=pltpu.CompilerParams(vmem_limit_bytes=vmem * 1024 * 1024),
    )(*args, *after)


def message_kernel(points, w_in, b_in, w_out, hi, lo):
    hidden = jax.nn.gelu(dot(points[...], w_in[...]) + b_in[...]).astype(BF)
    hi[...], lo[...] = split(dot(hidden, w_out[...]))


def partial_kernel(idx, hi, lo, out):
    codes = idx[...].astype(jnp.int16)
    rows, slots = codes.shape
    points = hi.shape[0]
    lane = lax.broadcasted_iota(jnp.int16, (rows, points), 1)
    one, zero = jnp.ones((), BF), jnp.zeros((), BF)
    counts = jnp.zeros((rows, points), BF)
    for j in range(slots):
        counts += jnp.where(codes[:, j : j + 1] == lane, one, zero)
    out[...] = (dot(counts, hi[...]) + dot(counts, lo[...])).astype(BF)


def pool_kernel(parts, count, b_out, pooled):
    rows = pooled.shape[0]
    total = jnp.zeros((rows, D), F32)
    for i in range(parts.shape[0] // rows):
        total += parts[i * rows : (i + 1) * rows, :].astype(F32)
    pooled[...] = (total / count[...] + b_out[...]).astype(BF)


def latent_query_kernel(pooled, gain, w, scale, out):
    normed = layer_norm(pooled[...], gain[...]).astype(BF)
    out[...] = (head_norm(dot(normed, w[...])) * scale[...]).astype(BF)


def query_kernel(rows, w, scale, out):
    out[...] = (head_norm(dot(rows[...], w[...])) * scale[...]).astype(BF)


def project_kernel(n, *refs):
    pieces = refs[:n]
    gain, wk, wv, keys, vals = refs[n:]
    keyed = [layer_norm(piece[...], gain[...]).astype(BF) for piece in pieces]
    keyed = jnp.concatenate(keyed, axis=0)
    keys[...] = head_norm(dot(keyed, wk[...])).astype(BF)
    vals[...] = dot(keyed, wv[...]).astype(BF)


def attend_kernel(q, keys, vals, own, part):
    nq = q.shape[0]
    half = nq // 2
    lane = lax.broadcasted_iota(jnp.int32, (1, 128), 1)
    low = lane < HEAD
    zero = jnp.zeros((), BF)
    ones = jnp.ones((keys.shape[0], 128), BF)
    den = jnp.zeros((nq, 128), F32)
    for pair in range(HEADS // 2):
        lanes = slice(pair * 128, pair * 128 + 128)
        q_pair = q[:, lanes]
        qs = jnp.concatenate([jnp.where(low, q_pair, zero), jnp.where(low, zero, q_pair)], axis=0)
        e = jnp.exp2(dot_nt(qs, keys[:, lanes])).astype(BF)
        found = dot(e, jnp.concatenate([vals[:, lanes], ones], axis=1))
        numer = jnp.where(low, found[:nq, :128], found[nq:, :128])
        own[:, lanes] = numer[:half]
        part[:, lanes] = numer[half:].astype(BF)
        den += jnp.where(lane == 2 * pair, found[:nq, 128:], 0.0)
        den += jnp.where(lane == 2 * pair + 1, found[nq:, 128:], 0.0)
    own[:, D:] = den[:half]
    part[:, D:] = den[half:].astype(BF)


def merged(whole):
    den = whole[:, D:]
    inverse = 1.0 / jnp.where(den > 0.0, den, 1.0)
    part = jnp.bitwise_and(lax.broadcasted_iota(jnp.int32, (256, D), 0), 127)
    head = lax.shift_right_logical(lax.broadcasted_iota(jnp.int32, (256, D), 1), 6)
    spread = jnp.where(part == head, 1.0, 0.0).astype(BF)
    return whole[:, :D] * dot(jnp.concatenate(split(inverse), axis=1), spread)


def mix_kernel(n, *refs):
    pooled, w, out = refs[n:]
    attended = merged(sum(p[...].astype(F32) for p in refs[:n])).astype(BF)
    out[...] = (pooled[...].astype(F32) + dot(attended, w[...])).astype(BF)


def head_kernel(own, part, ahead_lo, ahead_hi, behind_lo, behind_hi, gain, w, out):
    lo = ahead_lo[...].astype(F32) + behind_lo[...].astype(F32)
    hi = ahead_hi[...].astype(F32) + behind_hi[...].astype(F32)
    whole = own[...] + part[...].astype(F32) + jnp.concatenate([lo, hi], axis=0)
    rows = layer_norm(merged(whole), gain[...]).astype(BF)
    out[...] = dot_nt(w[...], rows)


def fetch(t, axis, ahead):
    n = SIZE[axis]
    return lax.ppermute(t, axis, [(i, (i - ahead) % n) for i in range(n)])


def gather_z(t):
    n = t.shape[0]
    after, before = fetch(t, "z", 1), fetch(t, "z", -1)
    three = jnp.concatenate([before, t, after], axis=0)
    far = fetch(three, "z", 3)
    back = fetch(three[n:], "z", -3)
    return jnp.concatenate([t, after, far, back, before], axis=0)


def ring(t, axis):
    return [t] + [fetch(t, axis, k) for k in range(1, SIZE[axis])]


def cat(pieces):
    return jnp.concatenate(pieces, axis=0)


def gather_rows(t):
    return ring(gather_z(t), "y")


SWAP = [(0, 1), (1, 0)]


def project(rows, gain, wk, wv, after=()):
    total = sum(r.shape[0] for r in rows)
    return call(
        functools.partial(project_kernel, len(rows)),
        [jax.ShapeDtypeStruct((total, D), BF)] * 2,
        *rows,
        gain,
        wk,
        wv,
        after=after,
        flops=4 * total * D * D,
    )


def attend(q, keys, vals, after=()):
    half = q.shape[0] // 2
    own, part = call(
        attend_kernel,
        [jax.ShapeDtypeStruct((half, D + 128), F32), jax.ShapeDtypeStruct((half, D + 128), BF)],
        q,
        keys,
        vals,
        after=after,
        flops=16 * q.shape[0] * keys.shape[0] * D,
    )
    return own, lax.ppermute(part, "c", SWAP)


def body(
    points,
    nbr_holder,
    nbr_local,
    nbr_count,
    w_in,
    b_in,
    w_out,
    b_out,
    gain_latent,
    w_query,
    w_key,
    w_value,
    w_mix,
    latent_temp,
    gain_keys,
    d_query,
    d_key,
    d_value,
    decoder_temp,
    gain_out,
    w_head,
    query_embed,
):
    rows_dev, slot_count = nbr_local.shape
    point_rows = points.shape[0]
    queries = query_embed.shape[0]
    z, c = lax.axis_index("z"), lax.axis_index("c")
    row = lambda v: v.reshape(1, -1)
    shape = jax.ShapeDtypeStruct

    live = lax.broadcasted_iota(jnp.int32, (rows_dev, slot_count), 1) < nbr_count[:, None]
    code = jnp.where(live, nbr_holder[:, :, 0] * point_rows + nbr_local, -1)
    other = lax.ppermute(code, "c", SWAP)
    chip = jnp.where(c == 0, cat([code, other]), cat([other, code]))
    slab = gather_z(chip)
    slab = lax.dynamic_slice_in_dim(cat([slab, slab]), (8 - z) % 8 * (2 * rows_dev), 16 * rows_dev, 0)
    first = (z * 2 + c) * point_rows
    idx = jnp.where((slab >= first) & (slab < first + point_rows), slab - first, -1)

    per_feature = lambda temp: row(jnp.repeat(temp * (LOG2E / HEAD), HEAD))
    dec_q = call(
        query_kernel,
        shape((queries, D), BF),
        query_embed,
        d_query,
        per_feature(decoder_temp),
        flops=2 * queries * D * D,
    )
    dec_q = cat([dec_q, lax.ppermute(dec_q, "c", SWAP)])
    ahead, behind = fetch(dec_q, "x", 1), fetch(dec_q, "x", -1)
    across = cat([fetch(ahead[:queries], "x", 1), fetch(behind[queries:], "x", -1)])

    hi, lo = call(
        message_kernel,
        [shape((point_rows, D), BF)] * 2,
        points,
        w_in,
        row(b_in),
        w_out,
        flops=4 * point_rows * D * D,
    )
    partial = call(
        partial_kernel, shape((16 * rows_dev, D), BF), idx, hi, lo, after=(dec_q,), flops=64 * rows_dev * point_rows * D
    )
    parts = lax.all_to_all(partial, ("z", "c"), split_axis=0, concat_axis=0, tiled=True)
    pooled = call(
        pool_kernel,
        shape((rows_dev, D), BF),
        parts,
        nbr_count.astype(F32)[:, None],
        row(b_out),
        after=(ahead, behind),
    )

    lat_q = call(
        latent_query_kernel,
        shape((rows_dev, D), BF),
        pooled,
        row(gain_latent),
        w_query,
        per_feature(latent_temp),
        flops=2 * rows_dev * D * D,
    )
    lat_q = cat(ring(lat_q, "x"))
    lat_q = cat([lat_q, lax.ppermute(lat_q, "c", SWAP)])
    keys, vals = project(gather_rows(pooled), row(gain_latent), w_key, w_value, after=(across,))
    own, part = attend(lat_q, keys, vals)
    both = own + part.astype(F32)
    block = lambda k: both[k * rows_dev : (k + 1) * rows_dev]
    found = [block(0)] + [fetch(block(k).astype(BF), "x", -k) for k in range(1, 4)]
    latent_out = call(
        functools.partial(mix_kernel, 4), shape((rows_dev, D), BF), *found, pooled, w_mix
    )

    keys, vals = project(gather_rows(latent_out), row(gain_keys), d_key, d_value)
    half = queries // 2
    own, part = attend(across, keys, vals)
    own_a, part_a = attend(ahead, keys, vals, after=(own,))
    far = (own + part.astype(F32)).astype(BF)
    onward = fetch(far[:half], "x", -1)
    back = fetch(far[half:], "x", 1)
    own_b, part_b = attend(behind, keys, vals, after=(far, own_a))
    own, part = attend(dec_q, keys, vals, after=(own_b,))
    own_a = own_a + part_a.astype(F32)
    own_b = own_b + part_b.astype(F32)
    ahead_hi = fetch(own_a[half:].astype(BF), "x", -1)
    behind_lo = fetch(own_b[:half].astype(BF), "x", 1)
    ahead_lo = fetch((own_a[:half] + onward.astype(F32)).astype(BF), "x", -1)
    behind_hi = fetch((own_b[half:] + back.astype(F32)).astype(BF), "x", 1)
    fields = call(
        head_kernel,
        shape((w_head.shape[0], queries), F32),
        own,
        part,
        ahead_lo,
        ahead_hi,
        behind_lo,
        behind_hi,
        row(gain_out),
        w_head,
    )
    return (latent_out, fields)


def solution(mesh):
    fine = Mesh(mesh.devices.reshape([SIZE[a] for a in AXES]), AXES)
    rows = P(AXES, None)
    placed = (rows, P(AXES, None, None), rows, P(AXES)) + (P(),) * 17 + (rows,)
    return jax.shard_map(
        body,
        mesh=fine,
        in_specs=placed,
        out_specs=(rows, P(None, AXES)),
        check_vma=False,
    )
```

```python
import functools

import jax
import jax.numpy as jnp
from jax import lax
from jax.experimental import pallas as pl
from jax.experimental.pallas import tpu as pltpu
from jax.sharding import Mesh, PartitionSpec as P

HEADS = 12
HEAD = 64
D = 768
LOG2E = 1.4426950408889634
AXES = ("y", "x", "z", "c")
SIZE = {"y": 4, "x": 4, "z": 8, "c": 2}
BF = jnp.bfloat16
F32 = jnp.float32


def dot(a, b):
    return jnp.dot(a, b, preferred_element_type=F32)


def dot_nt(a, b):
    return lax.dot_general(a, b, (((1,), (1,)), ((), ())), preferred_element_type=F32)


def split(x):
    hi = x.astype(BF)
    return hi, (x - hi.astype(F32)).astype(BF)


def head_norm(u):
    head = lax.shift_right_logical(lax.broadcasted_iota(jnp.int32, (D, 128), 0), 6)
    gather = jnp.where(head == lax.broadcasted_iota(jnp.int32, (D, 128), 1), 1.0, 0.0).astype(BF)
    ms = dot((u * u).astype(BF), gather) * (1.0 / HEAD)
    part = jnp.bitwise_and(lax.broadcasted_iota(jnp.int32, (256, D), 0), 127)
    head = lax.shift_right_logical(lax.broadcasted_iota(jnp.int32, (256, D), 1), 6)
    spread = jnp.where(part == head, 1.0, 0.0).astype(BF)
    return u * dot(jnp.concatenate(split(lax.rsqrt(ms + 1e-6)), axis=1), spread)


def layer_norm(x, gain):
    x = x.astype(F32)
    centred = x - jnp.mean(x, axis=-1, keepdims=True)
    spread = jnp.mean(centred * centred, axis=-1, keepdims=True)
    return centred * lax.rsqrt(spread + 1e-5) * gain


def call(kernel, out_shape, *args, after=(), smem=(), flops=0, vmem=48):
    specs = [
        pl.BlockSpec(memory_space=pltpu.SMEM if i in smem else pltpu.VMEM) for i in range(len(args))
    ]
    many = isinstance(out_shape, (list, tuple))
    out_specs = (
        [pl.BlockSpec(memory_space=pltpu.VMEM) for _ in out_shape]
        if many
        else pl.BlockSpec(memory_space=pltpu.VMEM)
    )
    specs += [pl.BlockSpec(memory_space=pl.ANY)] * len(after)
    nbytes = sum(a.size * a.dtype.itemsize for a in args)

    def run(*refs):
        kernel(*refs[: len(args)], *refs[len(args) + len(after) :])

    return pl.pallas_call(
        run,
        out_shape=out_shape,
        in_specs=specs,
        out_specs=out_specs,
        cost_estimate=pl.CostEstimate(flops=flops, bytes_accessed=nbytes, transcendentals=0),
        compiler_params=pltpu.CompilerParams(vmem_limit_bytes=vmem * 1024 * 1024),
    )(*args, *after)


def message_kernel(points, w_in, b_in, w_out, hi, lo):
    hidden = jax.nn.gelu(dot(points[...], w_in[...]) + b_in[...]).astype(BF)
    hi[...], lo[...] = split(dot(hidden, w_out[...]))


def partial_kernel(idx, hi, lo, out):
    codes = idx[...].astype(jnp.int16)
    rows, slots = codes.shape
    points = hi.shape[0]
    lane = lax.broadcasted_iota(jnp.int16, (rows, points), 1)
    one, zero = jnp.ones((), BF), jnp.zeros((), BF)
    counts = jnp.zeros((rows, points), BF)
    for j in range(slots):
        counts += jnp.where(codes[:, j : j + 1] == lane, one, zero)
    out[...] = (dot(counts, hi[...]) + dot(counts, lo[...])).astype(BF)


def pool_kernel(parts, count, b_out, pooled):
    rows = pooled.shape[0]
    total = jnp.zeros((rows, D), F32)
    for i in range(parts.shape[0] // rows):
        total += parts[i * rows : (i + 1) * rows, :].astype(F32)
    pooled[...] = (total / count[...] + b_out[...]).astype(BF)


def latent_query_kernel(pooled, gain, w, scale, out):
    normed = layer_norm(pooled[...], gain[...]).astype(BF)
    out[...] = (head_norm(dot(normed, w[...])) * scale[...]).astype(BF)


def query_kernel(rows, w, scale, out):
    out[...] = (head_norm(dot(rows[...], w[...])) * scale[...]).astype(BF)


def project_kernel(rows, gain, wk, wv, keys, vals):
    keyed = layer_norm(rows[...], gain[...]).astype(BF)
    keys[...] = head_norm(dot(keyed, wk[...])).astype(BF)
    vals[...] = dot(keyed, wv[...]).astype(BF)


def attend_kernel(n, q, *refs):
    keys, vals, (own, part) = refs[:n], refs[n : 2 * n], refs[2 * n :]
    total = sum(k.shape[0] for k in keys)
    nq = q.shape[0]
    half = nq // 2
    lane = lax.broadcasted_iota(jnp.int32, (1, 128), 1)
    low = lane < HEAD
    zero = jnp.zeros((), BF)
    ones = jnp.ones((total, 128), BF)
    den = jnp.zeros((nq, 128), F32)
    for pair in range(HEADS // 2):
        lanes = slice(pair * 128, pair * 128 + 128)
        q_pair = q[:, lanes]
        qs = jnp.concatenate([jnp.where(low, q_pair, zero), jnp.where(low, zero, q_pair)], axis=0)
        k_pair = jnp.concatenate([k[:, lanes] for k in keys], axis=0)
        v_pair = jnp.concatenate([v[:, lanes] for v in vals], axis=0)
        e = jnp.exp2(dot_nt(qs, k_pair)).astype(BF)
        found = dot(e, jnp.concatenate([v_pair, ones], axis=1))
        numer = jnp.where(low, found[:nq, :128], found[nq:, :128])
        own[:, lanes] = numer[:half]
        part[:, lanes] = numer[half:].astype(BF)
        den += jnp.where(lane == 2 * pair, found[:nq, 128:], 0.0)
        den += jnp.where(lane == 2 * pair + 1, found[nq:, 128:], 0.0)
    own[:, D:] = den[:half]
    part[:, D:] = den[half:].astype(BF)


def merged(whole):
    den = whole[:, D:]
    inverse = 1.0 / jnp.where(den > 0.0, den, 1.0)
    part = jnp.bitwise_and(lax.broadcasted_iota(jnp.int32, (256, D), 0), 127)
    head = lax.shift_right_logical(lax.broadcasted_iota(jnp.int32, (256, D), 1), 6)
    spread = jnp.where(part == head, 1.0, 0.0).astype(BF)
    return whole[:, :D] * dot(jnp.concatenate(split(inverse), axis=1), spread)


def mix_kernel(n, *refs):
    pooled, w, out = refs[n:]
    attended = merged(sum(p[...].astype(F32) for p in refs[:n])).astype(BF)
    out[...] = (pooled[...].astype(F32) + dot(attended, w[...])).astype(BF)


def head_kernel(own, part, ahead_lo, ahead_hi, behind_lo, behind_hi, gain, w, out):
    lo = ahead_lo[...].astype(F32) + behind_lo[...].astype(F32)
    hi = ahead_hi[...].astype(F32) + behind_hi[...].astype(F32)
    whole = own[...] + part[...].astype(F32) + jnp.concatenate([lo, hi], axis=0)
    rows = layer_norm(merged(whole), gain[...]).astype(BF)
    out[...] = dot_nt(w[...], rows)


def fetch(t, axis, ahead):
    n = SIZE[axis]
    return lax.ppermute(t, axis, [(i, (i - ahead) % n) for i in range(n)])


def gather_z(t):
    n = t.shape[0]
    after, before = fetch(t, "z", 1), fetch(t, "z", -1)
    three = jnp.concatenate([before, t, after], axis=0)
    far = fetch(three, "z", 3)
    back = fetch(three[n:], "z", -3)
    return jnp.concatenate([t, after, far, back, before], axis=0)


def ring(t, axis):
    return [t] + [fetch(t, axis, k) for k in range(1, SIZE[axis])]


def cat(pieces):
    return jnp.concatenate(pieces, axis=0)


def gather_rows(t):
    return ring(gather_z(t), "y")


SWAP = [(0, 1), (1, 0)]


def project(pieces, gain, wk, wv, after=()):
    last = len(pieces) - 1
    found = [
        call(
            project_kernel,
            [jax.ShapeDtypeStruct(rows.shape, BF)] * 2,
            rows,
            gain,
            wk,
            wv,
            after=after if i == last else (),
            flops=4 * rows.shape[0] * D * D,
        )
        for i, rows in enumerate(pieces)
    ]
    return [k for k, _ in found], [v for _, v in found]


def attend(q, keys, vals, after=()):
    half = q.shape[0] // 2
    own, part = call(
        functools.partial(attend_kernel, len(keys)),
        [jax.ShapeDtypeStruct((half, D + 128), F32), jax.ShapeDtypeStruct((half, D + 128), BF)],
        q,
        *keys,
        *vals,
        after=after,
        flops=64 * q.shape[0] * keys[0].shape[0] * D,
    )
    return own, lax.ppermute(part, "c", SWAP)


def body(
    points,
    nbr_holder,
    nbr_local,
    nbr_count,
    w_in,
    b_in,
    w_out,
    b_out,
    gain_latent,
    w_query,
    w_key,
    w_value,
    w_mix,
    latent_temp,
    gain_keys,
    d_query,
    d_key,
    d_value,
    decoder_temp,
    gain_out,
    w_head,
    query_embed,
):
    rows_dev, slot_count = nbr_local.shape
    point_rows = points.shape[0]
    queries = query_embed.shape[0]
    z, c = lax.axis_index("z"), lax.axis_index("c")
    row = lambda v: v.reshape(1, -1)
    shape = jax.ShapeDtypeStruct

    live = lax.broadcasted_iota(jnp.int32, (rows_dev, slot_count), 1) < nbr_count[:, None]
    code = jnp.where(live, nbr_holder[:, :, 0] * point_rows + nbr_local, -1)
    other = lax.ppermute(code, "c", SWAP)
    chip = jnp.where(c == 0, cat([code, other]), cat([other, code]))
    slab = gather_z(chip)
    slab = lax.dynamic_slice_in_dim(cat([slab, slab]), (8 - z) % 8 * (2 * rows_dev), 16 * rows_dev, 0)
    first = (z * 2 + c) * point_rows
    idx = jnp.where((slab >= first) & (slab < first + point_rows), slab - first, -1)

    per_feature = lambda temp: row(jnp.repeat(temp * (LOG2E / HEAD), HEAD))
    dec_q = call(
        query_kernel,
        shape((queries, D), BF),
        query_embed,
        d_query,
        per_feature(decoder_temp),
        flops=2 * queries * D * D,
    )
    dec_q = cat([dec_q, lax.ppermute(dec_q, "c", SWAP)])
    ahead, behind = fetch(dec_q, "x", 1), fetch(dec_q, "x", -1)
    across = cat([fetch(ahead[:queries], "x", 1), fetch(behind[queries:], "x", -1)])

    hi, lo = call(
        message_kernel,
        [shape((point_rows, D), BF)] * 2,
        points,
        w_in,
        row(b_in),
        w_out,
        flops=4 * point_rows * D * D,
    )
    partial = call(
        partial_kernel, shape((16 * rows_dev, D), BF), idx, hi, lo, after=(dec_q,), flops=64 * rows_dev * point_rows * D
    )
    parts = lax.all_to_all(partial, ("z", "c"), split_axis=0, concat_axis=0, tiled=True)
    pooled = call(
        pool_kernel,
        shape((rows_dev, D), BF),
        parts,
        nbr_count.astype(F32)[:, None],
        row(b_out),
        after=(ahead, behind),
    )

    lat_q = call(
        latent_query_kernel,
        shape((rows_dev, D), BF),
        pooled,
        row(gain_latent),
        w_query,
        per_feature(latent_temp),
        flops=2 * rows_dev * D * D,
    )
    lat_q = cat(ring(lat_q, "x"))
    lat_q = cat([lat_q, lax.ppermute(lat_q, "c", SWAP)])
    keys, vals = project(gather_rows(pooled), row(gain_latent), w_key, w_value, after=(across,))
    own, part = attend(lat_q, keys, vals)
    both = own + part.astype(F32)
    block = lambda k: both[k * rows_dev : (k + 1) * rows_dev]
    found = [block(0)] + [fetch(block(k).astype(BF), "x", -k) for k in range(1, 4)]
    latent_out = call(
        functools.partial(mix_kernel, 4), shape((rows_dev, D), BF), *found, pooled, w_mix
    )

    keys, vals = project(gather_rows(latent_out), row(gain_keys), d_key, d_value)
    half = queries // 2
    own, part = attend(across, keys, vals)
    own_a, part_a = attend(ahead, keys, vals, after=(own,))
    far = (own + part.astype(F32)).astype(BF)
    onward = fetch(far[:half], "x", -1)
    back = fetch(far[half:], "x", 1)
    own_b, part_b = attend(behind, keys, vals, after=(far, own_a))
    own, part = attend(dec_q, keys, vals, after=(own_b,))
    own_a = own_a + part_a.astype(F32)
    own_b = own_b + part_b.astype(F32)
    ahead_hi = fetch(own_a[half:].astype(BF), "x", -1)
    behind_lo = fetch(own_b[:half].astype(BF), "x", 1)
    ahead_lo = fetch((own_a[:half] + onward.astype(F32)).astype(BF), "x", -1)
    behind_hi = fetch((own_b[half:] + back.astype(F32)).astype(BF), "x", 1)
    fields = call(
        head_kernel,
        shape((w_head.shape[0], queries), F32),
        own,
        part,
        ahead_lo,
        ahead_hi,
        behind_lo,
        behind_hi,
        row(gain_out),
        w_head,
    )
    return (latent_out, fields)


def solution(mesh):
    fine = Mesh(mesh.devices.reshape([SIZE[a] for a in AXES]), AXES)
    rows = P(AXES, None)
    placed = (rows, P(AXES, None, None), rows, P(AXES)) + (P(),) * 17 + (rows,)
    return jax.shard_map(
        body,
        mesh=fine,
        in_specs=placed,
        out_specs=(rows, P(None, AXES)),
        check_vma=False,
    )
```
